256 devices in a mesh: expert: 16 (over z, core), tx: 8 (over y, x_hi), ty: 2 (over x_lo).
Axes of the slice: x: 4 (x_hi: 2, x_lo: 2; x = x_hi * 2 + x_lo), y: 4, z: 8, core: 2. Of those that a mesh axis runs over, the one named last changes fastest.
Arguments:
- tokens: bfloat16 [512, 128, 1664], P('expert', 'tx', 'ty'), may hold values from -6 to 6
- picks: int32 [16, 16], P('expert'), may hold values from 0 to 31
- combine: float32 [16, 16, 128], P('expert', None, 'tx'), may hold values from 0.05 to 1
- w_in: bfloat16 [16, 1664, 4096], P('expert', 'ty', 'tx'), may hold values from -0.15625 to 0.15625
- w_out: bfloat16 [16, 4096, 1664], P('expert', 'tx', 'ty'), may hold values from -0.09375 to 0.09375
- d_mixed: bfloat16 [512, 128, 1664], P('expert', 'tx', 'ty'), may hold values from -2 to 2
Outputs:
- mixed: bfloat16 [512, 128, 1664], P('expert', 'tx', 'ty')
- grad_tokens: bfloat16 [512, 128, 1664], P('expert', 'tx', 'ty')
- grad_combine: float32 [16, 16, 128], P('expert', None, 'tx')
- grad_w_in: float32 [16, 1664, 4096], P('expert', 'ty', 'tx')
- grad_w_out: float32 [16, 4096, 1664], P('expert', 'tx', 'ty')
The draws below stay inside these ranges and needn't reach their ends.
Inputs may be any that keep to these rules, and one draw needn't show every extreme that they name: `picks`: each expert takes exactly one block of every group; several experts may take the same block.
All inputs are finite; a program needn't handle non-finite values.
Results may differ from the reference program's by a relative error of at most 0.023.
Values may be sent and summed in bfloat16 or wider, within the bound.
No kernel may reach another device: no remote copies, remote signals or barrier semaphores. Data moves between devices by JAX's collectives and lax.ppermute only.
A program may use at most 128 MiB of HBM per device.

```python
import math
import jax
import jax.numpy as jnp
from jax import lax

D = 1664
FF = 4096
TILE = 128
BLK_GRP = 32
EXPERTS = 16
GROUPS = 16
NBLK = 512
N_TX = 8
N_TY = 2


def place_ends(result, own_key, least, high):
    index_at = [jax.random.randint(jax.random.fold_in(own_key, axis), (), 0, length) for axis, length in enumerate(result.shape)]
    widest = result.shape.index(max(result.shape))
    next_to = index_at[:widest] + [(index_at[widest] + 1) % result.shape[widest]] + index_at[widest + 1:]
    return result.at[tuple(index_at)].set(least).at[tuple(next_to)].set(high)


def block_levels(stream_key, extent, split, smallest, largest):
    factor_of, own = 1.0, jax.random.fold_in(stream_key, 6)
    for axis_at, parts in split:
        heights = jnp.exp(jax.random.uniform(jax.random.fold_in(own, axis_at), (parts,), jnp.float32, smallest / len(split), largest / len(split)))
        factor_of = factor_of * jnp.repeat(heights, extent[axis_at] // parts).reshape([-1 if axis == axis_at else 1 for axis in range(len(extent))])
    return factor_of


def centred(key, extent, width, most, cuts=(), kind=jnp.bfloat16):
    level = block_levels(key, extent, cuts, -0.22, 0.18) if cuts else 1.0
    values = jax.random.normal(key, extent, jnp.float32) * width * level
    return jnp.minimum(jnp.maximum(values, -most), most).astype(kind)


def setup_inputs(seed: int = 0) -> dict:
    arg_keys = jax.random.split(jax.random.key(seed), 7)
    return {
        "tokens": centred(arg_keys[0], (NBLK, TILE, D), 1.0, 6.0, ((0, 16), (1, 8), (2, 2))),
        "picks": place_ends(jax.random.randint(arg_keys[1], (GROUPS, EXPERTS), 0, BLK_GRP), jax.random.fold_in(arg_keys[1], 1), 0, BLK_GRP - 1).astype(jnp.int32),
        "combine": jnp.clip(jnp.exp(math.log(1.0) - 2.9957323 * jax.random.uniform(arg_keys[2], (GROUPS, EXPERTS, TILE), jnp.float32) ** block_levels(arg_keys[2], (GROUPS, EXPERTS, TILE), ((0, 16), (2, 8)), -0.2, 0.2)), 0.05, 1.0),
        "w_in": centred(arg_keys[3], (EXPERTS, D, FF), D ** -0.5, 0.15625, ((0, 16), (1, 2), (2, 8))),
        "w_out": centred(arg_keys[4], (EXPERTS, FF, D), FF ** -0.5, 0.09375, ((0, 16), (1, 8), (2, 2))),
        "d_mixed": centred(arg_keys[5], (NBLK, TILE, D), 0.3, 2.0, ((0, 16), (1, 8), (2, 2))),
    }


root_half = 0.7071067811865476
normal_peak = 0.3989422804014327


def gelu_value(values):
    return 0.5 * values * (1.0 + lax.erf(values * root_half))


def gelu_slope(values):
    return 0.5 * (1.0 + lax.erf(values * root_half)) + values * jnp.exp(-0.5 * values * values) * normal_peak


def piece_sum(operand, matrix, pieces):
    span = operand.shape[1] // pieces
    summed = jnp.zeros((operand.shape[0], matrix.shape[1]), jnp.float32)
    for position in range(pieces):
        partial_value = jnp.dot(operand[:, position * span:(position + 1) * span], matrix[position * span:(position + 1) * span], preferred_element_type=jnp.float32)
        summed = summed + lax.optimization_barrier(partial_value.astype(jnp.bfloat16)).astype(jnp.float32)
    return summed


def one_expert(operands):
    routed, routed_grad, first_weight, second_weight = operands
    flat_in = routed.reshape(-1, D)
    flat_grad = routed_grad.reshape(-1, D)
    pre_act = piece_sum(flat_in, first_weight, N_TY)
    hidden = gelu_value(pre_act).astype(jnp.bfloat16)
    output = piece_sum(hidden, second_weight, N_TX).astype(jnp.bfloat16)
    hidden_grad = piece_sum(flat_grad, second_weight.T, N_TY)
    pre_grad = (hidden_grad * gelu_slope(pre_act)).astype(jnp.bfloat16)
    grad_second = jnp.dot(hidden.T, flat_grad, preferred_element_type=jnp.float32)
    grad_first = jnp.dot(flat_in.T, pre_grad, preferred_element_type=jnp.float32)
    input_grad = piece_sum(pre_grad, first_weight.T, N_TX).astype(jnp.bfloat16)
    return output.reshape(GROUPS, TILE, D), grad_first, grad_second, input_grad.reshape(GROUPS, TILE, D)


def reference(tokens, picks, combine, w_in, w_out, d_mixed):
    blocks = (jnp.arange(GROUPS, dtype=jnp.int32)[:, None] * BLK_GRP + picks).astype(jnp.int32)
    flat_blocks = blocks.T.reshape(-1)
    routed_all = tokens[flat_blocks].reshape(EXPERTS, GROUPS, TILE, D)
    cotangent_all = d_mixed[flat_blocks].reshape(EXPERTS, GROUPS, TILE, D)
    scaling = jnp.transpose(combine, (1, 0, 2))[..., None]
    routed_grads = (scaling * cotangent_all.astype(jnp.float32)).astype(jnp.bfloat16)
    outputs, grad_w_in, grad_w_out, input_grads = lax.map(one_expert, (routed_all, routed_grads, w_in, w_out))
    weighted = (scaling * outputs.astype(jnp.float32)).reshape(EXPERTS * GROUPS, TILE, D)
    mixed = jnp.zeros((NBLK, TILE, D), jnp.float32).at[flat_blocks].add(weighted).astype(jnp.bfloat16)
    combine_sums = jnp.sum(cotangent_all.astype(jnp.float32) * outputs.astype(jnp.float32), axis=3)
    grad_combine = jnp.transpose(combine_sums, (1, 0, 2))
    grad_tokens = jnp.zeros((NBLK, TILE, D), jnp.float32).at[flat_blocks].add(input_grads.astype(jnp.float32).reshape(EXPERTS * GROUPS, TILE, D)).astype(jnp.bfloat16)
    return mixed, grad_tokens, grad_combine, grad_w_in, grad_w_out
```

```python
import jax
import jax.numpy as jnp
from jax import lax
from jax.experimental import pallas as pl
from jax.experimental.pallas import tpu as pltpu
from jax.sharding import PartitionSpec as P

root_half = 0.7071067811865476
normal_peak = 0.3989422804014327

BF = jnp.bfloat16
F32 = jnp.float32
VLIM = 48 * 1024 * 1024


def dot(a, b, ca, cb):
    return lax.dot_general(a, b, (((ca,), (cb,)), ((), ())), preferred_element_type=F32)


def shift(value, dy, flip):
    perm = [
        (y * 4 + x, ((y + dy) % 4) * 4 + (x ^ flip)) for y in range(4) for x in range(4)
    ]
    return lax.ppermute(value, ("tx", "ty"), perm)


def ring_gather(piece0, piece1):
    prev0, next1 = shift(piece0, 1, 0), shift(piece1, -1, 0)
    prev1, next0 = shift(piece1, 1, 0), shift(piece0, -1, 0)
    far0, far1 = shift(prev0, 1, 0), shift(next1, -1, 0)
    return [(piece0, piece1), (prev0, prev1), (next0, next1), (far0, far1)]


def gather_x(own):
    a = shift(own, 0, 1)
    b = shift(own, 0, 3)
    c = shift(own, 0, 2)
    return jnp.concatenate([own, c], 0), jnp.concatenate([a, b], 0)


def scatter_x(parts):
    half = parts[0].shape[0] // 2
    a = shift(parts[1][:half], 0, 1)
    b = shift(parts[1][half:], 0, 3)
    c = shift(parts[0][half:], 0, 2)
    total = parts[0][:half].astype(F32) + a.astype(F32) + b.astype(F32) + c.astype(F32)
    return total.astype(BF)


def up_kernel(x0, x1, *refs):
    w, (hid, slope) = refs[:-2], refs[-2:]
    a0, a1 = x0[...], x1[...]
    n = w[0].shape[1]
    for j in range(4):
        v = dot(a0, w[2 * j][...], 1, 0) + dot(a1, w[2 * j + 1][...], 1, 0)
        gate = 0.5 * (1.0 + lax.erf(v * root_half))
        hid[:, j * n : (j + 1) * n] = (v * gate).astype(BF)
        slope[:, j * n : (j + 1) * n] = gate + v * jnp.exp(-0.5 * v * v) * normal_peak


def up(x, w):
    rows, n = x[0].shape[0], w[0][0].shape[1] * 4
    return pl.pallas_call(
        up_kernel,
        out_shape=[jax.ShapeDtypeStruct((rows, n), BF), jax.ShapeDtypeStruct((rows, n), F32)],
        compiler_params=pltpu.CompilerParams(vmem_limit_bytes=VLIM),
        name="up",
    )(*x, *[p for b in w for p in b])


def down_kernel(g0, g1, hid, slope, *refs):
    w, (o0, o1, pre) = refs[:-3], refs[-3:]
    n = w[0].shape[0]
    b0, b1 = g0[...], g1[...]
    for j in range(4):
        hg = dot(b0, w[2 * j][...], 1, 1) + dot(b1, w[2 * j + 1][...], 1, 1)
        pre[:, j * n : (j + 1) * n] = (hg * slope[:, j * n : (j + 1) * n]).astype(BF)
    for d, o in ((0, o0), (1, o1)):
        acc = None
        for j in range(4):
            t = dot(hid[:, j * n : (j + 1) * n], w[2 * j + d][...], 1, 0)
            acc = t if acc is None else acc + t
        o[...] = acc.astype(BF)


def down(g, hid, slope, w):
    rows, cols = g[0].shape
    o = jax.ShapeDtypeStruct((rows, cols), BF)
    return pl.pallas_call(
        down_kernel,
        out_shape=[o, o, jax.ShapeDtypeStruct(hid.shape, BF)],
        compiler_params=pltpu.CompilerParams(vmem_limit_bytes=VLIM),
        name="down",
    )(*g, hid, slope, *[p for b in w for p in b])


def outer_kernel(lhs_t, g0, g1, *outs):
    n = outs[0].shape[0]
    for j in (3, 1, 2, 0):
        a = lhs_t[:, j * n : (j + 1) * n]
        for d, g in ((0, g0), (1, g1)):
            o = outs[2 * j + d]
            o[...] = dot(a, g[...], 0, 0).astype(o.dtype)


def grad_out(hid, g):
    n, cols = hid.shape[1] // 4, g[0].shape[1]
    o = [jax.ShapeDtypeStruct((n, cols), F32 if j == 0 else BF) for j in range(4) for d in range(2)]
    r = pl.pallas_call(
        outer_kernel,
        out_shape=o,
        compiler_params=pltpu.CompilerParams(vmem_limit_bytes=VLIM),
        name="grad_out",
    )(hid, *g)
    return [(r[2 * j], r[2 * j + 1]) for j in range(4)]


def inner_kernel(x0, x1, pre, *outs):
    n = outs[0].shape[1]
    for d, x in ((0, x0), (1, x1)):
        a = x[...]
        for j in (3, 1, 2, 0):
            o = outs[2 * j + d]
            o[...] = dot(a, pre[:, j * n : (j + 1) * n], 0, 0).astype(o.dtype)


def grad_in(x, pre):
    n, rows = pre.shape[1] // 4, x[0].shape[1]
    o = [jax.ShapeDtypeStruct((rows, n), F32 if j == 0 else BF) for j in range(4) for d in range(2)]
    r = pl.pallas_call(
        inner_kernel,
        out_shape=o,
        compiler_params=pltpu.CompilerParams(vmem_limit_bytes=VLIM),
        name="grad_in",
    )(*x, pre)
    return [(r[2 * j], r[2 * j + 1]) for j in range(4)]


def back_kernel(pre, *refs):
    w, (o0, o1) = refs[:-2], refs[-2:]
    n = w[0].shape[1]
    for d, o in ((0, o0), (1, o1)):
        acc = None
        for j in range(4):
            t = dot(pre[:, j * n : (j + 1) * n], w[2 * j + d][...], 1, 1)
            acc = t if acc is None else acc + t
        o[...] = acc.astype(BF)


def back(pre, w):
    o = jax.ShapeDtypeStruct((pre.shape[0], w[0][0].shape[0]), BF)
    return pl.pallas_call(
        back_kernel,
        out_shape=[o, o],
        compiler_params=pltpu.CompilerParams(vmem_limit_bytes=VLIM),
        name="back",
    )(pre, *[p for b in w for p in b])


def ring_scatter(blocks):
    own, prev, nxt, far = blocks
    a = shift(far[0], 1, 0)
    b = shift(far[1], -1, 0)
    n1 = shift(nxt[1], 1, 0)
    p0 = shift(prev[0], -1, 0)
    n0 = shift((nxt[0].astype(F32) + a.astype(F32)).astype(BF), 1, 0)
    p1 = shift((prev[1].astype(F32) + b.astype(F32)).astype(BF), -1, 0)
    s0 = own[0] + p0.astype(F32) + n0.astype(F32)
    s1 = own[1] + n1.astype(F32) + p1.astype(F32)
    return s0, s1


def body(tokens, picks, combine, w_in, w_out, d_mixed):
    chosen = picks[0]
    side = lax.axis_index("ty")
    wi, wo = w_in[0], w_out[0]
    half = wi.shape[1] // 2
    wi_keep = lax.dynamic_slice_in_dim(wi, side * half, half, 1)
    wi_give = lax.dynamic_slice_in_dim(wi, (1 - side) * half, half, 1)
    wo_keep = lax.dynamic_slice_in_dim(wo, side * half, half, 0)
    wo_give = lax.dynamic_slice_in_dim(wo, (1 - side) * half, half, 0)
    wi_other = shift(wi_give, 0, 1)
    wo_other = shift(wo_give, 0, 1)

    scaling = combine[0][:, :, None]
    picked_in = jnp.take(tokens, chosen, axis=0)
    picked_grad = jnp.take(d_mixed, chosen, axis=0)
    sent_grad = (scaling * picked_grad.astype(F32)).astype(BF)
    groups, tile, cols = picked_in.shape

    win = ring_gather(wi_keep, wi_other)
    x_own = lax.all_to_all(picked_in, "expert", 0, 0, tiled=True).reshape(groups * tile, cols)
    x = gather_x(x_own)
    wout = ring_gather(wo_keep, wo_other)
    g_own = lax.all_to_all(sent_grad, "expert", 0, 0, tiled=True).reshape(groups * tile, cols)
    g = gather_x(g_own)

    hid, slope = up(x, win)
    gwo = ring_scatter(grad_out(hid, g))
    o0, o1, pre = down(g, hid, slope, wout)
    out_sum = scatter_x((o0, o1)).reshape(groups, tile, cols)
    output_home = lax.all_to_all(out_sum, "expert", 0, 0, tiled=True)
    gwi = ring_scatter(grad_in(x, pre))
    in_sum = scatter_x(back(pre, win)).reshape(groups, tile, cols)
    input_home = lax.all_to_all(in_sum, "expert", 0, 0, tiled=True)

    gi_got = shift(gwi[1].astype(BF), 0, 1).astype(F32)
    go_got = shift(gwo[1].astype(BF), 0, 1).astype(F32)
    first = side == 0
    grad_first = jnp.concatenate(
        [jnp.where(first, gwi[0], gi_got), jnp.where(first, gi_got, gwi[0])], 1
    )
    grad_second = jnp.concatenate(
        [jnp.where(first, gwo[0], go_got), jnp.where(first, go_got, gwo[0])], 0
    )

    block_count = tokens.shape[0]
    onehot = (chosen[:, None] == jnp.arange(block_count, dtype=jnp.int32)[None, :]).astype(F32)
    mixed = jnp.einsum(
        "eb,etd->btd",
        onehot,
        scaling * output_home.astype(F32),
        precision=lax.Precision.HIGHEST,
    ).astype(BF)
    grad_tokens = jnp.einsum(
        "eb,etd->btd", onehot, input_home.astype(F32), precision=lax.Precision.HIGHEST
    ).astype(BF)
    combine_part = jnp.sum(picked_grad.astype(F32) * output_home.astype(F32), axis=2)
    grad_combine = combine_part + shift(combine_part, 0, 1)
    return (mixed, grad_tokens, grad_combine[None], grad_first[None], grad_second[None])


def solution(mesh):
    in_specs = (
        P("expert", "tx", "ty"),
        P("expert", None),
        P("expert", None, "tx"),
        P("expert", "ty", "tx"),
        P("expert", "tx", "ty"),
        P("expert", "tx", "ty"),
    )
    out_specs = (
        P("expert", "tx", "ty"),
        P("expert", "tx", "ty"),
        P("expert", None, "tx"),
        P("expert", "ty", "tx"),
        P("expert", "tx", "ty"),
    )
    return jax.shard_map(body, mesh=mesh, in_specs=in_specs, out_specs=out_specs, check_vma=False)
```

```python
import jax
import jax.numpy as jnp
from jax import lax
from jax.experimental import pallas as pl
from jax.experimental.pallas import tpu as pltpu
from jax.sharding import PartitionSpec as P

root_half = 0.7071067811865476
normal_peak = 0.3989422804014327

BF = jnp.bfloat16
F32 = jnp.float32
VLIM = 48 * 1024 * 1024


def dot(a, b, ca, cb):
    return lax.dot_general(a, b, (((ca,), (cb,)), ((), ())), preferred_element_type=F32)


def shift(value, dy, flip, what):
    perm = [
        (y * 4 + x, ((y + dy) % 4) * 4 + (x ^ flip)) for y in range(4) for x in range(4)
    ]
    with jax.named_scope(what):
        return lax.ppermute(value, ("tx", "ty"), perm)


def tie(value, *others):
    return lax.optimization_barrier((value,) + others)[0]


def ring_gather(own, what):
    prev = shift(own, 1, 0, what + "_prev")
    nxt = shift(own, -1, 0, what + "_next")
    half = own.shape[0] // 2
    far0 = shift(prev[:half], 1, 0, what + "_far0")
    far1 = shift(nxt[half:], -1, 0, what + "_far1")
    return [own, prev, nxt, far0, far1]


def gather_x(own, what):
    a = shift(own, 0, 1, what + "_col")
    b = shift(own, 0, 3, what + "_both")
    c = shift(own, 0, 2, what + "_row")
    return own, c, a, b


def scatter_x(parts, what):
    a = shift(parts[2], 0, 1, what + "_col")
    b = shift(parts[3], 0, 3, what + "_both")
    c = shift(parts[1], 0, 2, what + "_row")
    total = parts[0].astype(F32) + a.astype(F32) + b.astype(F32) + c.astype(F32)
    return total.astype(BF)


def params():
    return pltpu.CompilerParams(vmem_limit_bytes=VLIM)


def blocks(refs, axis):
    half = refs[0].shape[0] // 2
    r = [(w[:half, :], w[half:, :]) for w in refs[:3]]
    return r + [(refs[3][...], refs[4][...])]


def rows_of(refs):
    return (
        jnp.concatenate([refs[0][...], refs[1][...]], 0),
        jnp.concatenate([refs[2][...], refs[3][...]], 0),
    )


def up_kernel(*refs):
    (a0, a1), w, (hid, slope) = rows_of(refs[:4]), blocks(refs[4:9], 1), refs[9:]
    n = refs[4].shape[1]
    for j in range(4):
        v = dot(a0, w[j][0], 1, 0) + dot(a1, w[j][1], 1, 0)
        gate = 0.5 * (1.0 + lax.erf(v * root_half))
        hid[:, j * n : (j + 1) * n] = (v * gate).astype(BF)
        slope[:, j * n : (j + 1) * n] = gate + v * jnp.exp(-0.5 * v * v) * normal_peak


def up(x, w):
    rows, n = x[0].shape[0] * 2, w[0].shape[1] * 4
    return pl.pallas_call(
        up_kernel,
        out_shape=[jax.ShapeDtypeStruct((rows, n), BF), jax.ShapeDtypeStruct((rows, n), F32)],
        compiler_params=params(),
        name="up",
    )(*x, *w)


def down_kernel(*refs):
    (b0, b1), (hid, slope), w, pre, outs = (
        rows_of(refs[:4]),
        refs[4:6],
        blocks(refs[6:11], 0),
        refs[11],
        refs[12:],
    )
    n = refs[9].shape[1]
    for j in range(4):
        hg = dot(b0, w[j][0], 1, 0) + dot(b1, w[j][1], 1, 0)
        pre[:, j * n : (j + 1) * n] = (hg * slope[:, j * n : (j + 1) * n]).astype(BF)
    half = b0.shape[0] // 2
    for d in (1, 0):
        acc = None
        for j in range(4):
            t = dot(hid[:, j * n : (j + 1) * n], w[j][d], 1, 1)
            acc = t if acc is None else acc + t
        acc = acc.astype(BF)
        outs[2 * d][...] = acc[:half]
        outs[2 * d + 1][...] = acc[half:]


def down(g, hid, slope, w):
    o = jax.ShapeDtypeStruct(g[0].shape, BF)
    r = pl.pallas_call(
        down_kernel,
        out_shape=[jax.ShapeDtypeStruct(hid.shape, BF), o, o, o, o],
        compiler_params=params(),
        name="down",
    )(*g, hid, slope, *w)
    return r[0], r[1:]


def back_kernel(*refs):
    pre, w, outs = refs[0], blocks(refs[1:6], 1), refs[6:]
    n = refs[1].shape[1]
    half = pre.shape[0] // 2
    for d in (1, 0):
        acc = None
        for j in range(4):
            t = dot(pre[:, j * n : (j + 1) * n], w[j][d], 1, 1)
            acc = t if acc is None else acc + t
        acc = acc.astype(BF)
        outs[2 * d][...] = acc[:half]
        outs[2 * d + 1][...] = acc[half:]


def back(pre, w):
    o = jax.ShapeDtypeStruct((pre.shape[0] // 2, w[3].shape[0]), BF)
    return pl.pallas_call(
        back_kernel,
        out_shape=[o, o, o, o],
        compiler_params=params(),
        name="back",
    )(pre, *w)


def inner_kernel(pre, *refs):
    a, outs = rows_of(refs[:4]), refs[4:]
    n = pre.shape[1] // 4
    m = a[0].shape[1]
    for d in (0, 1):
        for j in (3, 1, 2, 0):
            v = dot(a[d], pre[:, j * n : (j + 1) * n], 0, 0)
            if j == 3:
                outs[3 + d][...] = v.astype(BF)
            else:
                outs[j][d * m : (d + 1) * m, :] = v.astype(outs[j].dtype)


def weight_grad(kernel, wide, acts, shape, name):
    full = (shape[0] * 2, shape[1])
    o = [jax.ShapeDtypeStruct(full, F32)] + [jax.ShapeDtypeStruct(full, BF)] * 2
    o += [jax.ShapeDtypeStruct(shape, BF)] * 2
    return pl.pallas_call(kernel, out_shape=o, compiler_params=params(), name=name)(wide, *acts)


def ring_far(parts, what):
    return shift(parts[3], 1, 0, what + "_far0"), shift(parts[4], -1, 0, what + "_far1")


def ring_near(parts, a, b, what):
    prev, nxt = parts[1:3]
    half = nxt.shape[0] // 2
    n_tot = jnp.concatenate([(nxt[:half].astype(F32) + a.astype(F32)).astype(BF), nxt[half:]], 0)
    p_tot = jnp.concatenate([prev[:half], (prev[half:].astype(F32) + b.astype(F32)).astype(BF)], 0)
    return shift(n_tot, 1, 0, what + "_next"), shift(p_tot, -1, 0, what + "_prev"), (n_tot, p_tot)


def ring_give(own, n_got, p_got, what):
    half = own.shape[0] // 2
    s1 = (own[half:] + n_got[half:].astype(F32) + p_got[half:].astype(F32)).astype(BF)
    s0 = own[:half] + n_got[:half].astype(F32) + p_got[:half].astype(F32)
    return s0, shift(s1, 0, 1, what + "_give"), s1


def join_kernel(side, s0, got, out):
    n = s0.shape[1]
    out[:, pl.ds(pl.multiple_of(side[0] * n, n), n)] = s0[...]
    out[:, pl.ds(pl.multiple_of((1 - side[0]) * n, n), n)] = got[...].astype(F32)


def join(side, s0, got):
    vm = pl.BlockSpec(memory_space=pltpu.VMEM)
    return pl.pallas_call(
        join_kernel,
        out_shape=jax.ShapeDtypeStruct((s0.shape[0], s0.shape[1] * 2), F32),
        in_specs=[pl.BlockSpec(memory_space=pltpu.SMEM), vm, vm],
        compiler_params=params(),
        name="join",
    )(side, s0, got)


def body(tokens, picks, combine, w_in, w_out, d_mixed):
    chosen = picks[0]
    side = lax.axis_index("ty")
    wi, wo = w_in[0], w_out[0].T
    half = wi.shape[1] // 2
    wi_keep = lax.dynamic_slice_in_dim(wi, side * half, half, 1)
    wi_give = lax.dynamic_slice_in_dim(wi, (1 - side) * half, half, 1)
    wo_keep = lax.dynamic_slice_in_dim(wo, side * half, half, 1)
    wo_give = lax.dynamic_slice_in_dim(wo, (1 - side) * half, half, 1)
    wi_other = shift(wi_give, 0, 1, "wi_flip")
    wo_other = shift(wo_give, 0, 1, "wo_flip")

    scaling = combine[0][:, :, None]
    picked_in = tokens.at[chosen].get(mode="promise_in_bounds")
    picked_grad = d_mixed.at[chosen].get(mode="promise_in_bounds")
    sent_grad = (scaling * picked_grad.astype(F32)).astype(BF)
    groups, tile, cols = picked_in.shape

    wi_full = jnp.concatenate([wi_keep, wi_other], 0)
    wo_full = jnp.concatenate([wo_keep, wo_other], 0)
    win = ring_gather(wi_full, "wi")
    x_own = lax.all_to_all(picked_in, "expert", 0, 0, tiled=True).reshape(groups * tile, cols)
    x = gather_x(x_own, "x")
    wout = ring_gather(wo_full, "wo")
    g_own = lax.all_to_all(sent_grad, "expert", 0, 0, tiled=True).reshape(groups * tile, cols)
    g = gather_x(g_own, "g")

    hid, slope = up(x, win)
    go = weight_grad(inner_kernel, hid, g, wo_keep.shape, "grad_out")
    go_a, go_b = ring_far(go, "go")
    pre, o = down(g, tie(hid, go[3]), slope, wout)
    go_n, go_p, n_tot = ring_near(go, tie(go_a, pre), go_b, "go")
    out_sum = scatter_x(o, "out").reshape(groups, tile, cols)
    gi = weight_grad(inner_kernel, tie(pre, *n_tot), x, wi_keep.shape, "grad_in")
    gi_a, gi_b = ring_far(gi, "gi")
    inp = back(tie(pre, gi[3]), win)
    go0, go_got, go_s = ring_give(go[0], tie(go_n, gi[3]), go_p, "go")
    gi_n, gi_p, gi_tot = ring_near(gi, tie(gi_a, go_s, inp[0]), gi_b, "gi")
    output_home = lax.all_to_all(out_sum, "expert", 0, 0, tiled=True)
    in_sum = scatter_x(inp, "inp").reshape(groups, tile, cols)
    input_home = lax.all_to_all(tie(in_sum, go_got), "expert", 0, 0, tiled=True)
    gi0, gi_got, _ = ring_give(gi[0], gi_n, gi_p, "gi")

    where = side.astype(jnp.int32).reshape(1)
    grad_first = join(where, gi0, gi_got)
    grad_second = join(where, go0, go_got).T

    block_count = tokens.shape[0]
    onehot = (chosen[:, None] == jnp.arange(block_count, dtype=jnp.int32)[None, :]).astype(F32)
    mixed = jnp.einsum(
        "eb,etd->btd",
        onehot,
        scaling * output_home.astype(F32),
        precision=lax.Precision.HIGHEST,
    ).astype(BF)
    grad_tokens = jnp.einsum(
        "eb,etd->btd", onehot, input_home.astype(F32), precision=lax.Precision.HIGHEST
    ).astype(BF)
    combine_part = jnp.sum(picked_grad.astype(F32) * output_home.astype(F32), axis=2)
    grad_combine = combine_part + shift(combine_part, 0, 1, "combine_part")
    return (mixed, grad_tokens, grad_combine[None], grad_first[None], grad_second[None])


def solution(mesh):
    in_specs = (
        P("expert", "tx", "ty"),
        P("expert", None),
        P("expert", None, "tx"),
        P("expert", "ty", "tx"),
        P("expert", "tx", "ty"),
        P("expert", "tx", "ty"),
    )
    out_specs = (
        P("expert", "tx", "ty"),
        P("expert", "tx", "ty"),
        P("expert", None, "tx"),
        P("expert", "ty", "tx"),
        P("expert", "tx", "ty"),
    )
    return jax.shard_map(body, mesh=mesh, in_specs=in_specs, out_specs=out_specs, check_vma=False)
```

```python
import jax
import jax.numpy as jnp
from jax import lax
from jax.experimental import pallas as pl
from jax.experimental.pallas import tpu as pltpu
from jax.sharding import PartitionSpec as P

root_half = 0.7071067811865476
normal_peak = 0.3989422804014327

BF = jnp.bfloat16
F32 = jnp.float32
VLIM = 48 * 1024 * 1024


def dot(a, b, ca, cb):
    return lax.dot_general(a, b, (((ca,), (cb,)), ((), ())), preferred_element_type=F32)


def shift(value, dy, flip, what):
    perm = [
        (y * 4 + x, ((y + dy) % 4) * 4 + (x ^ flip)) for y in range(4) for x in range(4)
    ]
    with jax.named_scope(what):
        return lax.ppermute(value, ("tx", "ty"), perm)


def tie(value, *others):
    return lax.optimization_barrier((value,) + others)[0]


def ring_gather(own, what):
    prev = shift(own, 1, 0, what + "_prev")
    nxt = shift(own, -1, 0, what + "_next")
    half = own.shape[0] // 2
    far0 = shift(prev[:half], 1, 0, what + "_far0")
    far1 = shift(nxt[half:], -1, 0, what + "_far1")
    return [own, prev, nxt, far0, far1]


def gather_x(own, what):
    a = shift(own, 0, 1, what + "_col")
    b = shift(own, 0, 3, what + "_both")
    c = shift(own, 0, 2, what + "_row")
    return own, c, a, b


def scatter_x(parts, what):
    a = shift(parts[2], 0, 1, what + "_col")
    b = shift(parts[3], 0, 3, what + "_both")
    c = shift(parts[1], 0, 2, what + "_row")
    total = parts[0].astype(F32) + a.astype(F32) + b.astype(F32) + c.astype(F32)
    return total.astype(BF)


def params():
    return pltpu.CompilerParams(vmem_limit_bytes=VLIM)


def blocks(refs, axis):
    half = refs[0].shape[0] // 2
    r = [(w[:half, :], w[half:, :]) for w in refs[:3]]
    return r + [(refs[3][...], refs[4][...])]


def rows_of(refs):
    return (
        jnp.concatenate([refs[0][...], refs[1][...]], 0),
        jnp.concatenate([refs[2][...], refs[3][...]], 0),
    )


def up_kernel(*refs):
    (a0, a1), w, (hid, slope) = rows_of(refs[:4]), blocks(refs[4:9], 1), refs[9:]
    n = refs[4].shape[1]
    for j in range(4):
        v = dot(a0, w[j][0], 1, 0) + dot(a1, w[j][1], 1, 0)
        gate = 0.5 * (1.0 + lax.erf(v * root_half))
        hid[:, j * n : (j + 1) * n] = (v * gate).astype(BF)
        slope[:, j * n : (j + 1) * n] = gate + v * jnp.exp(-0.5 * v * v) * normal_peak


def up(x, w):
    rows, n = x[0].shape[0] * 2, w[0].shape[1] * 4
    return pl.pallas_call(
        up_kernel,
        out_shape=[jax.ShapeDtypeStruct((rows, n), BF), jax.ShapeDtypeStruct((rows, n), F32)],
        compiler_params=params(),
        name="up",
    )(*x, *w)


def down_kernel(*refs):
    (b0, b1), (hid, slope), w, pre, outs = (
        rows_of(refs[:4]),
        refs[4:6],
        blocks(refs[6:11], 0),
        refs[11],
        refs[12:],
    )
    n = refs[9].shape[1]
    for j in range(4):
        hg = dot(b0, w[j][0], 1, 0) + dot(b1, w[j][1], 1, 0)
        pre[:, j * n : (j + 1) * n] = (hg * slope[:, j * n : (j + 1) * n]).astype(BF)
    half = b0.shape[0] // 2
    for d in (1, 0):
        acc = None
        for j in range(4):
            t = dot(hid[:, j * n : (j + 1) * n], w[j][d], 1, 1)
            acc = t if acc is None else acc + t
        acc = acc.astype(BF)
        outs[2 * d][...] = acc[:half]
        outs[2 * d + 1][...] = acc[half:]


def down(g, hid, slope, w):
    o = jax.ShapeDtypeStruct(g[0].shape, BF)
    r = pl.pallas_call(
        down_kernel,
        out_shape=[jax.ShapeDtypeStruct(hid.shape, BF), o, o, o, o],
        compiler_params=params(),
        name="down",
    )(*g, hid, slope, *w)
    return r[0], r[1:]


def back_kernel(*refs):
    pre, w, outs = refs[0], blocks(refs[1:6], 1), refs[6:]
    n = refs[1].shape[1]
    half = pre.shape[0] // 2
    for d in (1, 0):
        acc = None
        for j in range(4):
            t = dot(pre[:, j * n : (j + 1) * n], w[j][d], 1, 1)
            acc = t if acc is None else acc + t
        acc = acc.astype(BF)
        outs[2 * d][...] = acc[:half]
        outs[2 * d + 1][...] = acc[half:]


def back(pre, w):
    o = jax.ShapeDtypeStruct((pre.shape[0] // 2, w[3].shape[0]), BF)
    return pl.pallas_call(
        back_kernel,
        out_shape=[o, o, o, o],
        compiler_params=params(),
        name="back",
    )(pre, *w)


def inner_kernel(pre, *refs):
    a, outs = rows_of(refs[:4]), refs[4:]
    n = pre.shape[1] // 4
    m = a[0].shape[1]
    for d in (0, 1):
        for j in (3, 1, 2, 0):
            v = dot(a[d], pre[:, j * n : (j + 1) * n], 0, 0)
            if j == 3:
                outs[3 + d][...] = v.astype(BF)
            else:
                outs[j][d * m : (d + 1) * m, :] = v.astype(outs[j].dtype)


def weight_grad(kernel, wide, acts, shape, name):
    full = (shape[0] * 2, shape[1])
    o = [jax.ShapeDtypeStruct(full, F32)] + [jax.ShapeDtypeStruct(full, BF)] * 2
    o += [jax.ShapeDtypeStruct(shape, BF)] * 2
    return pl.pallas_call(kernel, out_shape=o, compiler_params=params(), name=name)(wide, *acts)


def ring_far(parts, what):
    return shift(parts[3], 1, 0, what + "_far0"), shift(parts[4], -1, 0, what + "_far1")


def ring_near(parts, a, b, what):
    prev, nxt = parts[1:3]
    half = nxt.shape[0] // 2
    n_tot = jnp.concatenate([(nxt[:half].astype(F32) + a.astype(F32)).astype(BF), nxt[half:]], 0)
    p_tot = jnp.concatenate([prev[:half], (prev[half:].astype(F32) + b.astype(F32)).astype(BF)], 0)
    return shift(n_tot, 1, 0, what + "_next"), shift(p_tot, -1, 0, what + "_prev"), (n_tot, p_tot)


def ring_give(own, n_got, p_got, what):
    half = own.shape[0] // 2
    s1 = (own[half:] + n_got[half:].astype(F32) + p_got[half:].astype(F32)).astype(BF)
    s0 = own[:half] + n_got[:half].astype(F32) + p_got[:half].astype(F32)
    return s0, shift(s1, 0, 1, what + "_give"), s1


def join_kernel(side, s0, got, out):
    n = s0.shape[1]
    out[:, pl.ds(pl.multiple_of(side[0] * n, n), n)] = s0[...]
    out[:, pl.ds(pl.multiple_of((1 - side[0]) * n, n), n)] = got[...].astype(F32)


def join(side, s0, got):
    vm = pl.BlockSpec(memory_space=pltpu.VMEM)
    return pl.pallas_call(
        join_kernel,
        out_shape=jax.ShapeDtypeStruct((s0.shape[0], s0.shape[1] * 2), F32),
        in_specs=[pl.BlockSpec(memory_space=pltpu.SMEM), vm, vm],
        compiler_params=params(),
        name="join",
    )(side, s0, got)


def body(tokens, picks, combine, w_in, w_out, d_mixed):
    chosen = picks[0]
    side = lax.axis_index("ty")
    wi, wo = w_in[0], w_out[0].T
    half = wi.shape[1] // 2
    wi_keep = lax.dynamic_slice_in_dim(wi, side * half, half, 1)
    wi_give = lax.dynamic_slice_in_dim(wi, (1 - side) * half, half, 1)
    wo_keep = lax.dynamic_slice_in_dim(wo, side * half, half, 1)
    wo_give = lax.dynamic_slice_in_dim(wo, (1 - side) * half, half, 1)
    wi_other = shift(wi_give, 0, 1, "wi_flip")
    wo_other = shift(wo_give, 0, 1, "wo_flip")

    scaling = combine[0][:, :, None]
    picked_in = tokens.at[chosen].get(mode="promise_in_bounds")
    picked_grad = d_mixed.at[chosen].get(mode="promise_in_bounds")
    sent_grad = (scaling * picked_grad.astype(F32)).astype(BF)
    groups, tile, cols = picked_in.shape

    wi_full = jnp.concatenate([wi_keep, wi_other], 0)
    wo_full = jnp.concatenate([wo_keep, wo_other], 0)
    win = ring_gather(wi_full, "wi")
    x_own = lax.all_to_all(picked_in, "expert", 0, 0, tiled=True).reshape(groups * tile, cols)
    x = gather_x(x_own, "x")
    wout = ring_gather(wo_full, "wo")
    g_own = lax.all_to_all(sent_grad, "expert", 0, 0, tiled=True).reshape(groups * tile, cols)
    g = gather_x(g_own, "g")

    hid, slope = up(x, win)
    go = weight_grad(inner_kernel, hid, g, wo_keep.shape, "grad_out")
    go_a, go_b = ring_far(go, "go")
    pre, o = down(g, tie(hid, go[3]), slope, wout)
    go_n, go_p, n_tot = ring_near(go, tie(go_a, pre), go_b, "go")
    out_sum = scatter_x(o, "out").reshape(groups, tile, cols)
    gi = weight_grad(inner_kernel, tie(pre, *n_tot), x, wi_keep.shape, "grad_in")
    gi_a, gi_b = ring_far(gi, "gi")
    inp = back(tie(pre, gi[3]), win)
    go0, go_got, go_s = ring_give(go[0], tie(go_n, gi[3]), go_p, "go")
    gi_n, gi_p, gi_tot = ring_near(gi, tie(gi_a, go_s, inp[0]), gi_b, "gi")
    output_home = lax.all_to_all(out_sum, "expert", 0, 0, tiled=True)
    in_sum = scatter_x(inp, "inp").reshape(groups, tile, cols)
    input_home = lax.all_to_all(tie(in_sum, go_s), "expert", 0, 0, tiled=True)
    gi0, gi_got, gi_s = ring_give(gi[0], tie(gi_n, go_got), gi_p, "gi")

    where = side.astype(jnp.int32).reshape(1)
    grad_first = join(where, gi0, gi_got)
    grad_second = join(where, go0, go_got).T

    block_count = tokens.shape[0]
    onehot = (chosen[:, None] == jnp.arange(block_count, dtype=jnp.int32)[None, :]).astype(F32)
    mixed = jnp.einsum(
        "eb,etd->btd",
        onehot,
        scaling * output_home.astype(F32),
        precision=lax.Precision.HIGHEST,
    ).astype(BF)
    grad_tokens = jnp.einsum(
        "eb,etd->btd", onehot, input_home.astype(F32), precision=lax.Precision.HIGHEST
    ).astype(BF)
    combine_part = jnp.sum(picked_grad.astype(F32) * output_home.astype(F32), axis=2)
    grad_combine = combine_part + shift(combine_part, 0, 1, "combine_part")
    return (mixed, grad_tokens, grad_combine[None], grad_first[None], grad_second[None])


def solution(mesh):
    in_specs = (
        P("expert", "tx", "ty"),
        P("expert", None),
        P("expert", None, "tx"),
        P("expert", "ty", "tx"),
        P("expert", "tx", "ty"),
        P("expert", "tx", "ty"),
    )
    out_specs = (
        P("expert", "tx", "ty"),
        P("expert", "tx", "ty"),
        P("expert", None, "tx"),
        P("expert", "ty", "tx"),
        P("expert", "tx", "ty"),
    )
    return jax.shard_map(body, mesh=mesh, in_specs=in_specs, out_specs=out_specs, check_vma=False)
```

```python
import jax
import jax.numpy as jnp
from jax import lax
from jax.experimental import pallas as pl
from jax.experimental.pallas import tpu as pltpu
from jax.sharding import PartitionSpec as P

root_half = 0.7071067811865476
normal_peak = 0.3989422804014327

BF = jnp.bfloat16
F32 = jnp.float32
VLIM = 48 * 1024 * 1024


def dot(a, b, ca, cb):
    return lax.dot_general(a, b, (((ca,), (cb,)), ((), ())), preferred_element_type=F32)


def shift(value, dy, flip, what):
    perm = [
        (y * 4 + x, ((y + dy) % 4) * 4 + (x ^ flip)) for y in range(4) for x in range(4)
    ]
    with jax.named_scope(what):
        return lax.ppermute(value, ("tx", "ty"), perm)


def tie(value, *others):
    return lax.optimization_barrier((value,) + others)[0]


def ring_gather(own, what):
    prev = shift(own, 1, 0, what + "_prev")
    nxt = shift(own, -1, 0, what + "_next")
    half = own.shape[0] // 2
    far0 = shift(prev[:half], 1, 0, what + "_far0")
    far1 = shift(nxt[half:], -1, 0, what + "_far1")
    return [own, prev, nxt, far0, far1]


def gather_x(own, what):
    a = shift(own, 0, 1, what + "_col")
    b = shift(own, 0, 3, what + "_both")
    c = shift(own, 0, 2, what + "_row")
    return own, c, a, b


def scatter_x(parts, what):
    a = shift(parts[2], 0, 1, what + "_col")
    b = shift(parts[3], 0, 3, what + "_both")
    c = shift(parts[1], 0, 2, what + "_row")
    total = parts[0].astype(F32) + a.astype(F32) + b.astype(F32) + c.astype(F32)
    return total.astype(BF)


def params():
    return pltpu.CompilerParams(vmem_limit_bytes=VLIM)


def blocks(refs, axis):
    half = refs[0].shape[0] // 2
    r = [(w[:half, :], w[half:, :]) for w in refs[:3]]
    return r + [(refs[3][...], refs[4][...])]


def rows_of(refs):
    return (
        jnp.concatenate([refs[0][...], refs[1][...]], 0),
        jnp.concatenate([refs[2][...], refs[3][...]], 0),
    )


def up_kernel(*refs):
    (a0, a1), w, (hid, slope) = rows_of(refs[:4]), blocks(refs[4:9], 1), refs[9:]
    n = refs[4].shape[1]
    for j in range(4):
        v = dot(a0, w[j][0], 1, 0) + dot(a1, w[j][1], 1, 0)
        gate = 0.5 * (1.0 + lax.erf(v * root_half))
        hid[:, j * n : (j + 1) * n] = (v * gate).astype(BF)
        slope[:, j * n : (j + 1) * n] = gate + v * jnp.exp(-0.5 * v * v) * normal_peak


def up(x, w):
    rows, n = x[0].shape[0] * 2, w[0].shape[1] * 4
    return pl.pallas_call(
        up_kernel,
        out_shape=[jax.ShapeDtypeStruct((rows, n), BF), jax.ShapeDtypeStruct((rows, n), F32)],
        compiler_params=params(),
        name="up",
    )(*x, *w)


def down_kernel(*refs):
    (b0, b1), (hid, slope), w, pre, outs = (
        rows_of(refs[:4]),
        refs[4:6],
        blocks(refs[6:11], 0),
        refs[11],
        refs[12:],
    )
    n = refs[9].shape[1]
    for j in range(4):
        hg = dot(b0, w[j][0], 1, 0) + dot(b1, w[j][1], 1, 0)
        pre[:, j * n : (j + 1) * n] = (hg * slope[:, j * n : (j + 1) * n]).astype(BF)
    half = b0.shape[0] // 2
    for d in (1, 0):
        acc = None
        for j in range(4):
            t = dot(hid[:, j * n : (j + 1) * n], w[j][d], 1, 1)
            acc = t if acc is None else acc + t
        acc = acc.astype(BF)
        outs[2 * d][...] = acc[:half]
        outs[2 * d + 1][...] = acc[half:]


def down(g, hid, slope, w):
    o = jax.ShapeDtypeStruct(g[0].shape, BF)
    r = pl.pallas_call(
        down_kernel,
        out_shape=[jax.ShapeDtypeStruct(hid.shape, BF), o, o, o, o],
        compiler_params=params(),
        name="down",
    )(*g, hid, slope, *w)
    return r[0], r[1:]


def back_kernel(*refs):
    pre, w, outs = refs[0], blocks(refs[1:6], 1), refs[6:]
    n = refs[1].shape[1]
    half = pre.shape[0] // 2
    for d in (1, 0):
        acc = None
        for j in range(4):
            t = dot(pre[:, j * n : (j + 1) * n], w[j][d], 1, 1)
            acc = t if acc is None else acc + t
        acc = acc.astype(BF)
        outs[2 * d][...] = acc[:half]
        outs[2 * d + 1][...] = acc[half:]


def back(pre, w):
    o = jax.ShapeDtypeStruct((pre.shape[0] // 2, w[3].shape[0]), BF)
    return pl.pallas_call(
        back_kernel,
        out_shape=[o, o, o, o],
        compiler_params=params(),
        name="back",
    )(pre, *w)


def inner_kernel(pre, *refs):
    a, outs = rows_of(refs[:4]), refs[4:]
    n = pre.shape[1] // 4
    m = a[0].shape[1]
    for d in (0, 1):
        for j in (3, 1, 2, 0):
            v = dot(a[d], pre[:, j * n : (j + 1) * n], 0, 0)
            if j == 3:
                outs[3 + d][...] = v.astype(BF)
            else:
                outs[j][d * m : (d + 1) * m, :] = v.astype(outs[j].dtype)


def weight_grad(kernel, wide, acts, shape, name):
    full = (shape[0] * 2, shape[1])
    o = [jax.ShapeDtypeStruct(full, F32)] + [jax.ShapeDtypeStruct(full, BF)] * 2
    o += [jax.ShapeDtypeStruct(shape, BF)] * 2
    return pl.pallas_call(kernel, out_shape=o, compiler_params=params(), name=name)(wide, *acts)


def ring_far(parts, what):
    return shift(parts[3], 1, 0, what + "_far0"), shift(parts[4], -1, 0, what + "_far1")


def ring_near(parts, a, b, what):
    prev, nxt = parts[1:3]
    half = nxt.shape[0] // 2
    n_tot = jnp.concatenate([(nxt[:half].astype(F32) + a.astype(F32)).astype(BF), nxt[half:]], 0)
    p_tot = jnp.concatenate([prev[:half], (prev[half:].astype(F32) + b.astype(F32)).astype(BF)], 0)
    return shift(n_tot, 1, 0, what + "_next"), shift(p_tot, -1, 0, what + "_prev"), (n_tot, p_tot)


def ring_give(own, n_got, p_got, what):
    half = own.shape[0] // 2
    s1 = (own[half:] + n_got[half:].astype(F32) + p_got[half:].astype(F32)).astype(BF)
    s0 = own[:half] + n_got[:half].astype(F32) + p_got[:half].astype(F32)
    return s0, shift(s1, 0, 1, what + "_give"), s1


def join_kernel(side, s0, got, out):
    n = s0.shape[1]
    out[:, pl.ds(pl.multiple_of(side[0] * n, n), n)] = s0[...]
    out[:, pl.ds(pl.multiple_of((1 - side[0]) * n, n), n)] = got[...].astype(F32)


def join(side, s0, got):
    vm = pl.BlockSpec(memory_space=pltpu.VMEM)
    return pl.pallas_call(
        join_kernel,
        out_shape=jax.ShapeDtypeStruct((s0.shape[0], s0.shape[1] * 2), F32),
        in_specs=[pl.BlockSpec(memory_space=pltpu.SMEM), vm, vm],
        compiler_params=params(),
        name="join",
    )(side, s0, got)


def body(tokens, picks, combine, w_in, w_out, d_mixed):
    chosen = picks[0]
    side = lax.axis_index("ty")
    wi, wo = w_in[0], w_out[0].T
    half = wi.shape[1] // 2
    wi_keep = lax.dynamic_slice_in_dim(wi, side * half, half, 1)
    wi_give = lax.dynamic_slice_in_dim(wi, (1 - side) * half, half, 1)
    wo_keep = lax.dynamic_slice_in_dim(wo, side * half, half, 1)
    wo_give = lax.dynamic_slice_in_dim(wo, (1 - side) * half, half, 1)
    wi_other = shift(wi_give, 0, 1, "wi_flip")
    wo_other = shift(wo_give, 0, 1, "wo_flip")

    scaling = combine[0][:, :, None]
    picked_in = tokens.at[chosen].get(mode="promise_in_bounds")
    picked_grad = d_mixed.at[chosen].get(mode="promise_in_bounds")
    sent_grad = (scaling * picked_grad.astype(F32)).astype(BF)
    groups, tile, cols = picked_in.shape

    wi_full = jnp.concatenate([wi_keep, wi_other], 0)
    wo_full = jnp.concatenate([wo_keep, wo_other], 0)
    win = ring_gather(wi_full, "wi")
    x_own = lax.all_to_all(picked_in, "expert", 0, 0, tiled=True).reshape(groups * tile, cols)
    x = gather_x(x_own, "x")
    wout = ring_gather(wo_full, "wo")
    g_own = lax.all_to_all(sent_grad, "expert", 0, 0, tiled=True).reshape(groups * tile, cols)
    g = gather_x(g_own, "g")

    hid, slope = up(x, win)
    go = weight_grad(inner_kernel, hid, g, wo_keep.shape, "grad_out")
    go_a, go_b = ring_far(go, "go")
    pre, o = down(g, tie(hid, go[3]), slope, wout)
    go_n, go_p, n_tot = ring_near(go, tie(go_a, pre), go_b, "go")
    out_sum = scatter_x(o, "out").reshape(groups, tile, cols)
    gi = weight_grad(inner_kernel, tie(pre, *n_tot), x, wi_keep.shape, "grad_in")
    gi_a, gi_b = ring_far(gi, "gi")
    inp = back(tie(pre, gi[3]), win)
    gi_n, gi_p, gi_tot = ring_near(gi, tie(gi_a, go_n, go_p, inp[0]), gi_b, "gi")
    go0, go_got, go_s = ring_give(go[0], tie(go_n, *gi_tot), go_p, "go")
    output_home = lax.all_to_all(out_sum, "expert", 0, 0, tiled=True)
    in_sum = scatter_x(inp, "inp").reshape(groups, tile, cols)
    input_home = lax.all_to_all(tie(in_sum, go_s), "expert", 0, 0, tiled=True)
    gi0, gi_got, gi_s = ring_give(gi[0], tie(gi_n, go_got), gi_p, "gi")

    where = side.astype(jnp.int32).reshape(1)
    grad_first = join(where, gi0, gi_got)
    grad_second = join(where, go0, go_got).T

    block_count = tokens.shape[0]
    onehot = (chosen[:, None] == jnp.arange(block_count, dtype=jnp.int32)[None, :]).astype(F32)
    mixed = jnp.einsum(
        "eb,etd->btd",
        onehot,
        scaling * output_home.astype(F32),
        precision=lax.Precision.HIGHEST,
    ).astype(BF)
    grad_tokens = jnp.einsum(
        "eb,etd->btd", onehot, input_home.astype(F32), precision=lax.Precision.HIGHEST
    ).astype(BF)
    combine_part = jnp.sum(picked_grad.astype(F32) * output_home.astype(F32), axis=2)
    grad_combine = combine_part + shift(combine_part, 0, 1, "combine_part")
    return (mixed, grad_tokens, grad_combine[None], grad_first[None], grad_second[None])


def solution(mesh):
    in_specs = (
        P("expert", "tx", "ty"),
        P("expert", None),
        P("expert", None, "tx"),
        P("expert", "ty", "tx"),
        P("expert", "tx", "ty"),
        P("expert", "tx", "ty"),
    )
    out_specs = (
        P("expert", "tx", "ty"),
        P("expert", "tx", "ty"),
        P("expert", None, "tx"),
        P("expert", "ty", "tx"),
        P("expert", "tx", "ty"),
    )
    return jax.shard_map(body, mesh=mesh, in_specs=in_specs, out_specs=out_specs, check_vma=False)
```
